32 devices in a mesh: section: 2 (over y), expert: 16 (over z, x, core).
Axes of the slice: x: 2, y: 2, z: 4, core: 2. Of those that a mesh axis runs over, the one named last changes fastest.
Arguments:
- front_rows: bfloat16 [2, 512, 1024], P('section', 'expert'), may hold values from -25 to 25
- front_routes: int32 [2, 512, 8], P('section', 'expert'), may hold values from 0 to 15, all different within a row; in each aligned block of 32 rows (0 to 31, 32 to 63, ..., all dimensions but the last counted through in order) at most 17 rows name the same one
- front_weights: float32 [2, 512, 8], P('section', 'expert'), may hold values from 0.1 to 1
- rear_rows: bfloat16 [2, 512, 1024], P('section', 'expert'), may hold values from -25 to 25
- rear_routes: int32 [2, 512, 8], P('section', 'expert'), may hold values from 0 to 15, all different within a row; in each aligned block of 32 rows (0 to 31, 32 to 63, ..., all dimensions but the last counted through in order) at most 17 rows name the same one
- rear_weights: float32 [2, 512, 8], P('section', 'expert'), may hold values from 0.1 to 1
- rear_cotangent: bfloat16 [2, 512, 1024], P('section', 'expert'), may hold values from -6 to 6
- norm_gain: float32 [2, 1024], P('section'), may hold values from 0.25 to 1.75
- gate_weight: bfloat16 [2, 16, 1024, 512], P('section', 'expert'), may hold values from -0.1875 to 0.1875
- up_weight: bfloat16 [2, 16, 1024, 512], P('section', 'expert'), may hold values from -0.1875 to 0.1875
- down_weight: bfloat16 [2, 16, 512, 1024], P('section', 'expert'), may hold values from -0.25 to 0.25
Outputs:
- sent_ahead: bfloat16 [2, 512, 1024], P('section', 'expert')
- sent_behind: bfloat16 [2, 512, 1024], P('section', 'expert')
The draws below stay inside these ranges and needn't reach their ends.
Inputs may be any that keep to these rules, and one draw needn't show every extreme that they name: `front_routes`: A token's 8 experts differ; within each section's aligned blocks of 32 tokens no expert is chosen by more than 17 tokens, a bound that some block reaches. `rear_routes`: A token's 8 experts differ; within each section's aligned blocks of 32 tokens no expert is chosen by more than 17 tokens, a bound that some block reaches.
All inputs are finite; a program needn't handle non-finite values.
Results may differ from the reference program's by a relative error of at most 0.0065.
Values may be sent and summed in bfloat16 or wider, within the bound.
No kernel may reach another device: no remote copies, remote signals or barrier semaphores. Data moves between devices by JAX's collectives and lax.ppermute only.
A program may use at most 64 MiB of HBM per device.

```python
import math
import jax
import jax.numpy as jnp
import numpy as np
from jax import lax

D = 1024
FF = 512
TOPK = 8
TOK_DEV = 32
EXPERTS = 16
CAP = 17
SECTIONS = 2
TOKENS = 512
N_EXPERT = 16


def scaled_rows(key):
    key_rows = jax.random.fold_in(key, 11)
    key_cols = jax.random.fold_in(key, 12)
    key_base = jax.random.fold_in(key, 13)
    row_scale = jnp.power(10.0, jax.random.uniform(key_rows, (SECTIONS, TOKENS, 1), jnp.float32, -0.5, 0.5))
    col_scale = jnp.power(10.0, jax.random.uniform(key_cols, (1, 1, D), jnp.float32, -0.5, 0.5))
    base = jnp.clip(jax.random.normal(key_base, (SECTIONS, TOKENS, D), jnp.float32), -2.4, 2.4)
    return (base * row_scale * col_scale).astype(jnp.bfloat16)


def draw_front_rows(key, part):
    return scaled_rows(jax.random.fold_in(key, 101))


def draw_rear_rows(key, part):
    return scaled_rows(jax.random.fold_in(key, 202))


def steps_of(key, dims, pieces, smallest, top_value):
    loudness, own = 1.0, jax.random.fold_in(key, 6)
    for dim, parts in pieces:
        steps = jnp.exp(jax.random.uniform(jax.random.fold_in(own, dim), (parts,), jnp.float32, smallest / len(pieces), top_value / len(pieces)))
        loudness = loudness * jnp.repeat(steps, dims[dim] // parts).reshape([-1 if axis == dim else 1 for axis in range(len(dims))])
    return loudness


def routed_block(stream_key, own, number, rows, amount, top, bound, slope):
    order = jax.random.permutation(stream_key, amount)
    crowded, ordinary = load_shares(amount, rows * top, bound, slope, True), load_shares(amount, rows * top, bound, slope, False)
    places = jnp.arange(amount)

    def named(lengths, offset_by):
        used = int((lengths > 0).sum())
        fixed = max(1, used // 4)
        moved = fixed + (places - fixed + offset_by * (used - fixed)) % max(1, amount - fixed)
        return jnp.zeros((amount,), jnp.int32).at[order[jnp.where(places < fixed, places, moved)]].set(jnp.asarray(lengths, jnp.int32))

    lengths = jnp.where(number % 4 == 0, named(crowded, number // 4), named(ordinary, number - number // 4 - 1))
    mixed = jax.random.permutation(jax.random.fold_in(own, 3), amount)
    donor, receiver = mixed[0:amount // 2 * 2:2], mixed[1:amount // 2 * 2:2]
    room = jnp.minimum(lengths[donor] - 1, bound - lengths[receiver]) // 2
    room = jnp.where((donor == order[0]) | (receiver == order[0]) | (lengths[receiver] == 0), 0, jnp.maximum(room, 0))
    moved = jax.random.randint(jax.random.fold_in(own, 4), (amount // 2,), 0, 1 << 20) % (room + 1)
    lengths = lengths.at[donor].add(-moved).at[receiver].add(moved)
    items = jnp.searchsorted(jnp.cumsum(lengths), jnp.arange(rows * top), side="right").astype(jnp.int32)
    grid = items.reshape(top, rows).T
    grid = grid[jax.random.permutation(jax.random.fold_in(own, 1), rows)]
    offset_by = jax.random.randint(jax.random.fold_in(own, 2), (rows, 1), 0, top)
    return jnp.take_along_axis(grid, (jnp.arange(top)[None, :] + offset_by) % top, axis=1)


def load_shares(amount, total, most, lean, full):
    loads = [(1 << 20) // math.isqrt(rank ** lean) + 1 for rank in range(1, amount + 1)]
    largest = most if full else min(most, max(-(-total // amount), total * loads[0] // sum(loads)))
    least = 1 if total - largest >= amount - 1 else 0
    given, rest = [largest] + [least] * (amount - 1), total - largest - least * (amount - 1)
    while rest > 0:
        candidates = [i for i in range(1, amount) if given[i] < largest] or [i for i in range(1, amount) if given[i] < most]
        whole, left = sum([loads[i] for i in candidates]), rest
        for i in candidates:
            more = min(most - given[i], max(1, left * loads[i] // whole), rest)
            given[i] = given[i] + more
            rest = rest - more
    return np.array(given)


def centred(own_key, shape, scale, reach, pieces=(), kind=jnp.bfloat16):
    loudness = steps_of(own_key, shape, pieces, -0.22, 0.18) if pieces else 1.0
    result = jax.random.normal(own_key, shape, jnp.float32) * scale * loudness
    return jnp.minimum(jnp.maximum(result, -reach), reach).astype(kind)


def setup_inputs(seed: int = 0) -> dict:
    keys = jax.random.split(jax.random.key(seed), 12)
    front_rows = draw_front_rows(jax.random.fold_in(keys[11], 71), 0)
    front_routes_keys = jax.random.split(jax.random.fold_in(keys[1], 1), SECTIONS * TOKENS // TOK_DEV)
    front_routes_turns = jax.random.permutation(jax.random.fold_in(keys[1], 3), SECTIONS * TOKENS // TOK_DEV)
    front_routes = jax.vmap(lambda own, number: routed_block(jax.random.fold_in(keys[1], 2), own, number, TOK_DEV, EXPERTS, TOPK, CAP, 2))(front_routes_keys, front_routes_turns).reshape((SECTIONS, TOKENS, TOPK))
    front_weights = jnp.clip(0.1 + 0.9 * jax.random.uniform(keys[2], (SECTIONS, TOKENS, TOPK), jnp.float32) ** steps_of(keys[2], (SECTIONS, TOKENS, TOPK), ((0, 2), (1, 16)), -0.2, 0.2), 0.1, 1.0)
    rear_rows = draw_rear_rows(jax.random.fold_in(keys[11], 71), 0)
    rear_routes_keys = jax.random.split(jax.random.fold_in(keys[4], 1), SECTIONS * TOKENS // TOK_DEV)
    rear_routes_turns = jax.random.permutation(jax.random.fold_in(keys[4], 3), SECTIONS * TOKENS // TOK_DEV)
    rear_routes = jax.vmap(lambda own, number: routed_block(jax.random.fold_in(keys[4], 2), own, number, TOK_DEV, EXPERTS, TOPK, CAP, 2))(rear_routes_keys, rear_routes_turns).reshape((SECTIONS, TOKENS, TOPK))
    rear_weights = jnp.clip(0.1 + 0.9 * jax.random.uniform(keys[5], (SECTIONS, TOKENS, TOPK), jnp.float32) ** steps_of(keys[5], (SECTIONS, TOKENS, TOPK), ((0, 2), (1, 16)), -0.2, 0.2), 0.1, 1.0)
    rear_cotangent = centred(keys[6], (SECTIONS, TOKENS, D), 1.0, 6.0, ((0, 2), (1, 16)))
    norm_gain = jnp.clip(1.0 + 0.15 * jax.random.normal(keys[7], (SECTIONS, D), jnp.float32), 0.25, 1.75)
    gate_weight = centred(keys[8], (SECTIONS, EXPERTS, D, FF), D ** -0.5, 0.1875, ((0, 2), (1, 16)))
    up_weight = centred(keys[9], (SECTIONS, EXPERTS, D, FF), D ** -0.5, 0.1875, ((0, 2), (1, 16)))
    down_weight = centred(keys[10], (SECTIONS, EXPERTS, FF, D), FF ** -0.5, 0.25, ((0, 2), (1, 16)))
    return dict(front_rows=front_rows, front_routes=front_routes, front_weights=front_weights, rear_rows=rear_rows, rear_routes=rear_routes, rear_weights=rear_weights, rear_cotangent=rear_cotangent, norm_gain=norm_gain, gate_weight=gate_weight, up_weight=up_weight, down_weight=down_weight)


epsilon = 1e-06

def slot_tables(routing, mixing):
    onehot = (routing[:, :, None] == jnp.arange(EXPERTS, dtype=jnp.int32)[None, None, :]).astype(jnp.int32)
    counts = lax.optimization_barrier(jnp.sum(onehot, axis=1))
    before = jnp.cumsum(counts, axis=0) - counts
    slot_rank = lax.optimization_barrier(jnp.sum(onehot * before[:, None, :], axis=2))
    position = (slot_rank[:, :, None] == jnp.arange(CAP, dtype=jnp.int32)[None, None, :]).astype(jnp.int32)
    assign = onehot[:, :, :, None] * position[:, :, None, :]
    chosen = lax.optimization_barrier(jnp.sum(assign, axis=1)).astype(jnp.float32)
    spread = lax.optimization_barrier(jnp.sum(assign.astype(jnp.float32) * mixing[:, :, None, None], axis=1))
    return (chosen, spread)

def normalize(token_rows, gain_row):
    widened = token_rows.astype(jnp.float32)
    inverse = lax.rsqrt(lax.optimization_barrier(jnp.mean(widened * widened, axis=-1, keepdims=True)) + epsilon)
    return ((widened * inverse * gain_row).astype(jnp.bfloat16), inverse)

def expert_forward(slot_rows, gate_matrix, up_matrix, down_matrix):
    gate_value = jnp.dot(slot_rows, gate_matrix, preferred_element_type=jnp.float32)
    up_value = jnp.dot(slot_rows, up_matrix, preferred_element_type=jnp.float32)
    hidden = (jax.nn.silu(gate_value) * up_value).astype(jnp.bfloat16)
    return jnp.dot(hidden, down_matrix, preferred_element_type=jnp.float32).astype(jnp.bfloat16)

def expert_backward(slot_rows, slot_grads, gate_matrix, up_matrix, down_matrix):
    gate_value = jnp.dot(slot_rows, gate_matrix, preferred_element_type=jnp.float32)
    up_value = jnp.dot(slot_rows, up_matrix, preferred_element_type=jnp.float32)
    gate_sigmoid = jax.nn.sigmoid(gate_value)
    gate_silu = gate_value * gate_sigmoid
    hidden_grad = jnp.dot(slot_grads, down_matrix.T, preferred_element_type=jnp.float32)
    gate_grad = (hidden_grad * up_value * gate_sigmoid * (1.0 + gate_value * (1.0 - gate_sigmoid))).astype(jnp.bfloat16)
    up_grad = (hidden_grad * gate_silu).astype(jnp.bfloat16)
    input_grad = jnp.dot(gate_grad, gate_matrix.T, preferred_element_type=jnp.float32)
    input_grad = input_grad + jnp.dot(up_grad, up_matrix.T, preferred_element_type=jnp.float32)
    return input_grad.astype(jnp.bfloat16)

def forward_item(item):
    return expert_forward(item[0], item[1], item[2], item[3])

def backward_item(item):
    return expert_backward(item[0], item[1], item[2], item[3], item[4])

def section_pass(items):
    front_rows, front_routes, front_weights, rear_rows, rear_routes, rear_weights, rear_cotangent, gain_row, gate_section, up_section, down_section = items
    blocks = N_EXPERT
    highest = lax.Precision.HIGHEST
    front_chosen, front_spread = jax.vmap(slot_tables)(front_routes.reshape(blocks, TOK_DEV, TOPK), front_weights.reshape(blocks, TOK_DEV, TOPK))
    rear_chosen, rear_spread = jax.vmap(slot_tables)(rear_routes.reshape(blocks, TOK_DEV, TOPK), rear_weights.reshape(blocks, TOK_DEV, TOPK))
    front_norm, front_inverse = normalize(front_rows, gain_row)
    rear_norm, rear_inverse = normalize(rear_rows, gain_row)
    front_slots = jnp.einsum('ptec,ptd->epcd', front_chosen, front_norm.reshape(blocks, TOK_DEV, D).astype(jnp.float32)).astype(jnp.bfloat16)
    front_out = lax.map(forward_item, (front_slots.reshape(EXPERTS, blocks * CAP, D), gate_section, up_section, down_section))
    front_out = front_out.reshape(EXPERTS, blocks, CAP, D)
    front_mix = jnp.einsum('ptec,epcd->ptd', front_spread, front_out.astype(jnp.float32), precision=highest)
    front_result = (front_rows.astype(jnp.float32) + front_mix.reshape(TOKENS, D)).astype(jnp.bfloat16)
    rear_slots = jnp.einsum('ptec,ptd->epcd', rear_chosen, rear_norm.reshape(blocks, TOK_DEV, D).astype(jnp.float32)).astype(jnp.bfloat16)
    grad_slots = jnp.einsum('ptec,ptd->epcd', rear_spread, rear_cotangent.reshape(blocks, TOK_DEV, D).astype(jnp.float32), precision=highest).astype(jnp.bfloat16)
    rear_back = lax.map(backward_item, (rear_slots.reshape(EXPERTS, blocks * CAP, D), grad_slots.reshape(EXPERTS, blocks * CAP, D), gate_section, up_section, down_section))
    rear_back = rear_back.reshape(EXPERTS, blocks, CAP, D)
    slot_sum = jnp.einsum('ptec,epcd->ptd', rear_chosen, rear_back.astype(jnp.float32), precision=highest)
    norm_grad = gain_row * slot_sum.reshape(TOKENS, D)
    widened = rear_rows.astype(jnp.float32)
    cubed = rear_inverse * rear_inverse * rear_inverse
    rear_result = rear_cotangent.astype(jnp.float32) + rear_inverse * norm_grad
    rear_result = rear_result - widened * cubed * lax.optimization_barrier(jnp.mean(widened * norm_grad, axis=-1, keepdims=True))
    return (front_result, rear_result.astype(jnp.bfloat16))

def reference(front_rows, front_routes, front_weights, rear_rows, rear_routes, rear_weights, rear_cotangent, norm_gain, gate_weight, up_weight, down_weight):
    front_all, rear_all = lax.map(section_pass, (front_rows, front_routes, front_weights, rear_rows, rear_routes, rear_weights, rear_cotangent, norm_gain, gate_weight, up_weight, down_weight))
    return (jnp.roll(front_all, 1, axis=0), jnp.roll(rear_all, -1, axis=0))
```

```python
import functools

import jax
import jax.numpy as jnp
from jax import lax
from jax.experimental import pallas as pl
from jax.experimental.pallas import tpu as pltpu
from jax.sharding import PartitionSpec as P

epsilon = 1e-06
F32 = jnp.float32
BF16 = jnp.bfloat16
VMEM_LIMIT = 32 * 1024 * 1024


def call(kernel, name, shapes, *operands, scalars=0, flops=0):
    vmem = pl.BlockSpec(memory_space=pltpu.VMEM)
    smem = pl.BlockSpec(memory_space=pltpu.SMEM)
    shapes = [jax.ShapeDtypeStruct(shape, dtype) for shape, dtype in shapes]
    moved = sum(value.size * value.dtype.itemsize for value in [*operands, *shapes])
    return pl.pallas_call(
        kernel,
        out_shape=shapes,
        in_specs=[smem] * scalars + [vmem] * (len(operands) - scalars),
        out_specs=[vmem] * len(shapes),
        compiler_params=pltpu.CompilerParams(vmem_limit_bytes=VMEM_LIMIT),
        cost_estimate=pl.CostEstimate(flops=flops, bytes_accessed=moved, transcendentals=0),
        name=name,
    )(*operands)


def ring_of(experts):
    chips = experts // 2
    return list(range(0, chips, 2)) + list(range(1, chips, 2))[::-1]


def ring_pairs(experts, by):
    ring = ring_of(experts)
    chips = len(ring)
    return [
        (2 * ring[i] + c, 2 * ring[(i + by) % chips] + c) for i in range(chips) for c in range(2)
    ]


def table_lanes(experts):
    return -(-4 * experts // 128) * 128


def pack_kernel(experts, fr, frt, fw, rr, rrt, rw, ct, gain, msg):
    tokens, width = fr.shape
    lanes = table_lanes(experts)
    for j, rows in ((0, fr), (1, rr)):
        wide = rows[...].astype(F32)
        inverse = lax.rsqrt(jnp.mean(wide * wide, axis=-1, keepdims=True) + epsilon)
        msg[:, j * width : (j + 1) * width] = (wide * inverse * gain[...]).astype(BF16)
    msg[:, 2 * width : 3 * width] = ct[...]
    row = lax.broadcasted_iota(jnp.int32, (lanes, tokens), 0)
    table = jnp.zeros((lanes, tokens), F32)
    for group, (routes, weights) in enumerate(((frt, fw), (frt, fw), (rrt, rw), (rrt, rw))):
        for k in range(routes.shape[0]):
            hit = row == routes[k : k + 1, :] + group * experts
            weight = weights[k : k + 1, :]
            high = weight.astype(BF16).astype(F32)
            table = table + jnp.where(hit, high if group % 2 == 0 else weight - high, 0.0)
    msg[:, 3 * width :] = table.T.astype(BF16)


def sigmoid(v):
    return 1.0 / (1.0 + jnp.exp(-v))


def expert_kernel(experts, me, *refs):
    *parts, gate, up, down, gain, own, other = refs
    width = gate.shape[0]
    lanes = table_lanes(experts)
    expert = me[0]
    rows = jnp.concatenate([part[:, : 3 * width] for part in parts], axis=0)
    table = jnp.concatenate([part[:, 3 * width :] for part in parts], axis=0).astype(F32)
    lane = lax.broadcasted_iota(jnp.int32, table.shape, 1)
    mixing = []
    for j in range(2):
        hit = (lane == expert + 2 * j * experts) | (lane == expert + (2 * j + 1) * experts)
        mixing.append(jnp.sum(jnp.where(hit, table, 0.0), axis=-1, keepdims=True))
    across = (((1,), (1,)), ((), ()))

    def dot(a, b):
        return jnp.dot(a, b, preferred_element_type=F32)

    def dot_t(a, b):
        return lax.dot_general(a, b, across, preferred_element_type=F32)

    half = rows.shape[0] // 2

    def put(at, value):
        own[:, at : at + width] = value[:half].astype(own.dtype)
        other[:, at : at + width] = value[half:].astype(other.dtype)

    front, rear, cotangent = (rows[:, j * width : (j + 1) * width] for j in range(3))
    gate_value = dot(front, gate[...])
    up_value = dot(front, up[...])
    hidden = (gate_value * sigmoid(gate_value) * up_value).astype(BF16)
    put(0, dot(hidden, down[...]) * mixing[0])
    gate_value = dot(rear, gate[...])
    up_value = dot(rear, up[...])
    hidden_grad = dot_t(cotangent, down[...]) * mixing[1]
    g = sigmoid(gate_value)
    gate_grad = (hidden_grad * up_value * g * (1.0 + gate_value * (1.0 - g))).astype(BF16)
    up_grad = (hidden_grad * gate_value * g).astype(BF16)
    put(width, (dot_t(gate_grad, gate[...]) + dot_t(up_grad, up[...])) * gain[...])


def home_kernel(own, other, fr, rr, ct, out):
    width = fr.shape[1]
    total = own[...] + other[...].astype(F32)
    out[:, :width] = (fr[...].astype(F32) + total[:, :width]).astype(BF16)
    out[:, width : 2 * width] = total[:, width:].astype(BF16)
    out[:, 2 * width : 3 * width] = rr[...]
    out[:, 3 * width :] = ct[...]


def finish_kernel(home, below, above, front, rear):
    width = front.shape[1]
    total = home[:, : 2 * width].astype(F32) + below[...].astype(F32) + above[...].astype(F32)
    front[...] = total[:, :width].astype(BF16)
    wide = home[:, 2 * width : 3 * width].astype(F32)
    inverse = lax.rsqrt(jnp.mean(wide * wide, axis=-1, keepdims=True) + epsilon)
    grad = total[:, width:]
    along = jnp.mean(wide * grad, axis=-1, keepdims=True)
    cubed = inverse * inverse * inverse
    cotangent = home[:, 3 * width :].astype(F32)
    rear[...] = (cotangent + inverse * grad - wide * cubed * along).astype(BF16)


def shards(
    front_rows,
    front_routes,
    front_weights,
    rear_rows,
    rear_routes,
    rear_weights,
    rear_cotangent,
    norm_gain,
    gate_weight,
    up_weight,
    down_weight,
):
    experts = lax.axis_size("expert")
    sections = lax.axis_size("section")
    tokens, width = front_rows.shape[1:]
    half = tokens // 2
    reach = experts // 4
    lanes = table_lanes(experts)
    up_pairs, down_pairs = ring_pairs(experts, 1), ring_pairs(experts, -1)
    twin_pairs = [(i, i ^ 1) for i in range(experts)]

    def twin(value):
        return lax.ppermute(value, "expert", twin_pairs)

    def both(upward, downward):
        return (
            lax.ppermute(upward, "expert", up_pairs),
            lax.ppermute(downward, "expert", down_pairs),
        )

    def across(value, pairs):
        def shifted(part, by):
            moves = [
                (s * experts + a, (s + by) % sections * experts + b)
                for s in range(sections)
                for a, b in pairs
            ]
            return lax.ppermute(part, ("section", "expert"), moves)

        if sections == 2:
            return shifted(value, 1)
        parts = [shifted(value[:, :width], 1), shifted(value[:, width:], -1)]
        return jnp.concatenate(parts, axis=1)

    (message,) = call(
        functools.partial(pack_kernel, experts),
        "pack",
        [((tokens, 3 * width + lanes), BF16)],
        front_rows[0],
        front_routes[0].T,
        front_weights[0].T,
        rear_rows[0],
        rear_routes[0].T,
        rear_weights[0].T,
        rear_cotangent[0],
        norm_gain,
    )
    me = lax.axis_index("expert").reshape(1)

    def expert_of(*mine):
        rows = sum(part.shape[0] for part in mine)
        own, other = call(
            functools.partial(expert_kernel, experts),
            "expert",
            [((rows, 2 * width), F32), ((rows, 2 * width), BF16)],
            me,
            *mine,
            *[twin(part) for part in mine],
            gate_weight[0, 0],
            up_weight[0, 0],
            down_weight[0, 0],
            norm_gain,
            scalars=1,
            flops=2 * 2 * rows * 8 * gate_weight[0, 0].size,
        )
        return own, twin(other)

    below, above = message, message
    results = [expert_of(message)]
    for step in range(1, reach):
        below, above = both(below, above)
        results.append(expert_of(below, above))
    far_below, far_above = both(below[:half], above[half:])
    results.append(expert_of(far_below, far_above))

    def total(step):
        own, other = results[step]
        return own + other.astype(F32)

    (home,) = call(
        home_kernel,
        "home",
        [((tokens, 4 * width), BF16)],
        *results[0],
        front_rows[0],
        rear_rows[0],
        rear_cotangent[0],
    )
    home = across(home, [(i, i) for i in range(experts)])
    far = total(reach).astype(BF16)
    from_below, from_above = both(far[:half], far[half:])
    for step in range(reach - 1, 0, -1):
        one = total(step)
        to_below, to_above = one[:tokens], one[tokens:]
        if step == reach - 1:
            to_above = jnp.concatenate(
                [to_above[:half] + from_below.astype(F32), to_above[half:]], axis=0
            )
            to_below = jnp.concatenate(
                [to_below[:half], to_below[half:] + from_above.astype(F32)], axis=0
            )
        else:
            to_above = to_above + from_below.astype(F32)
            to_below = to_below + from_above.astype(F32)
        to_below, to_above = to_below.astype(BF16), to_above.astype(BF16)
        if step > 1:
            from_below, from_above = both(to_above, to_below)
    from_below, from_above = across(to_above, up_pairs), across(to_below, down_pairs)
    front, rear = call(
        finish_kernel, "finish", [((tokens, width), BF16)] * 2, home, from_below, from_above
    )
    return (front[None], rear[None])


def solution(mesh):
    rows = P("section", "expert", None)
    weights = P("section", "expert", None, None)
    placed = (rows,) * 7 + (P("section", None),) + (weights,) * 3
    return jax.shard_map(
        shards, mesh=mesh, in_specs=placed, out_specs=(rows, rows), check_vma=False
    )
```

```python
import functools

import jax
import jax.numpy as jnp
from jax import lax
from jax.experimental import pallas as pl
from jax.experimental.pallas import tpu as pltpu
from jax.sharding import PartitionSpec as P

epsilon = 1e-06
F32 = jnp.float32
BF16 = jnp.bfloat16
VMEM_LIMIT = 16 * 1024 * 1024
PACK_LIMIT = 60 * 1024 * 1024
HOLD_LIMIT = 50 * 1024 * 1024


def call(kernel, name, shapes, *operands, scalars=0, flops=0, limit=VMEM_LIMIT, scratch=(), anywhere=()):
    vmem = pl.BlockSpec(memory_space=pltpu.VMEM)
    smem = pl.BlockSpec(memory_space=pltpu.SMEM)
    places = [smem] * scalars + [vmem] * (len(operands) - scalars)
    for at in anywhere:
        places[at] = pl.BlockSpec(memory_space=pltpu.HBM)
    shapes = [jax.ShapeDtypeStruct(shape, dtype) for shape, dtype in shapes]
    moved = sum(value.size * value.dtype.itemsize for value in [*operands, *shapes])
    return pl.pallas_call(
        kernel,
        out_shape=shapes,
        in_specs=places,
        out_specs=[vmem] * len(shapes),
        scratch_shapes=scratch,
        compiler_params=pltpu.CompilerParams(vmem_limit_bytes=limit),
        cost_estimate=pl.CostEstimate(flops=flops, bytes_accessed=moved, transcendentals=0),
        name=name,
    )(*operands)


def ring_of(experts):
    chips = experts // 2
    return list(range(0, chips, 2)) + list(range(1, chips, 2))[::-1]


def ring_pairs(experts, by):
    ring = ring_of(experts)
    chips = len(ring)
    return [
        (2 * ring[i] + c, 2 * ring[(i + by) % chips] + c) for i in range(chips) for c in range(2)
    ]


def table_lanes(experts):
    return -(-4 * experts // 128) * 128


def pack_kernel(experts, fr, frt, fw, rr, rrt, rw, ct, gain, msg, rest):
    tokens, width = fr.shape
    lanes = table_lanes(experts)
    for j, rows in ((0, fr), (1, rr)):
        wide = rows[...].astype(F32)
        inverse = lax.rsqrt(jnp.mean(wide * wide, axis=-1, keepdims=True) + epsilon)
        msg[:, j * width : (j + 1) * width] = (wide * inverse * gain[...]).astype(BF16)
    msg[:, 2 * width : 3 * width] = ct[...]
    for j, rows in enumerate((fr, rr, ct)):
        rest[:, j * width : (j + 1) * width] = rows[...]
    row = lax.broadcasted_iota(jnp.int32, (lanes, tokens), 0)
    table = jnp.zeros((lanes, tokens), F32)
    for group, (routes, weights) in enumerate(((frt, fw), (frt, fw), (rrt, rw), (rrt, rw))):
        for k in range(routes.shape[0]):
            hit = row == routes[k : k + 1, :] + group * experts
            weight = weights[k : k + 1, :]
            high = weight.astype(BF16).astype(F32)
            table = table + jnp.where(hit, high if group % 2 == 0 else weight - high, 0.0)
    msg[:, 3 * width :] = table.T.astype(BF16)


def sigmoid(v):
    return 1.0 / (1.0 + jnp.exp(-v))


def hold_kernel(*refs):
    *refs, sems = refs
    count = len(refs) // 2
    copies = [
        pltpu.make_async_copy(refs[i], refs[count + i], sems.at[i]) for i in range(count)
    ]
    for copy in copies:
        copy.start()
    for copy in copies:
        copy.wait()


def expert_kernel(experts, *refs):
    *parts, gate, up, down, gate_twin, up_twin, down_twin, gain, out = refs
    width = gate.shape[0]
    rows = jnp.concatenate([part[:, : 3 * width] for part in parts], axis=0)
    table = jnp.concatenate([part[:, 3 * width :] for part in parts], axis=0).astype(F32)
    lane = lax.broadcasted_iota(jnp.int32, table.shape, 1)
    count = rows.shape[0]
    across = (((1,), (1,)), ((), ()))

    def mixing(expert, group):
        hit = (lane == expert + group * experts) | (lane == expert + (group + 1) * experts)
        return jnp.sum(jnp.where(hit, table, 0.0), axis=-1, keepdims=True)

    def dot(a, b):
        return jnp.dot(a, b, preferred_element_type=F32)

    def dot_t(a, b):
        return lax.dot_general(a, b, across, preferred_element_type=F32)

    both_rows = jnp.concatenate([rows[:, :width], rows[:, width : 2 * width]], axis=0)
    cotangent = rows[:, 2 * width :]
    me = lax.axis_index("expert")
    front = rear = 0.0
    for expert, gate, up, down in (
        (me, gate, up, down),
        (me ^ 1, gate_twin, up_twin, down_twin),
    ):
        gate_value = dot(both_rows, gate[...])
        up_value = dot(both_rows, up[...])
        g = sigmoid(gate_value)
        silu = gate_value * g
        hidden = (silu[:count] * up_value[:count]).astype(BF16)
        front = front + dot(hidden, down[...]) * mixing(expert, 0)
        gate_value, up_value, g, silu = (v[count:] for v in (gate_value, up_value, g, silu))
        hidden_grad = dot_t(cotangent, down[...]) * mixing(expert, 2)
        gate_grad = (hidden_grad * up_value * g * (1.0 + gate_value * (1.0 - g))).astype(BF16)
        up_grad = (hidden_grad * silu).astype(BF16)
        rear = rear + dot_t(gate_grad, gate[...]) + dot_t(up_grad, up[...])
    out[:, :width] = front
    out[:, width:] = rear * gain[...]


def finish_kernel(rest, home, far, below, above, front, rear):
    width = front.shape[1]
    total = home[...].astype(F32) + far[...].astype(F32)
    total = total + below[...].astype(F32) + above[...].astype(F32)
    front[...] = (rest[:, :width].astype(F32) + total[:, :width]).astype(BF16)
    wide = rest[:, width : 2 * width].astype(F32)
    inverse = lax.rsqrt(jnp.mean(wide * wide, axis=-1, keepdims=True) + epsilon)
    grad = total[:, width:]
    along = jnp.mean(wide * grad, axis=-1, keepdims=True)
    cubed = inverse * inverse * inverse
    cotangent = rest[:, 2 * width :].astype(F32)
    rear[...] = (cotangent + inverse * grad - wide * cubed * along).astype(BF16)


def shards(
    front_rows,
    front_routes,
    front_weights,
    rear_rows,
    rear_routes,
    rear_weights,
    rear_cotangent,
    norm_gain,
    gate_weight,
    up_weight,
    down_weight,
):
    experts = lax.axis_size("expert")
    sections = lax.axis_size("section")
    tokens, width = front_rows.shape[1:]
    half = tokens // 2
    reach = experts // 4
    lanes = table_lanes(experts)
    up_pairs, down_pairs = ring_pairs(experts, 1), ring_pairs(experts, -1)
    twin_pairs = [(i, i ^ 1) for i in range(experts)]

    def both(upward, downward):
        return (
            lax.ppermute(upward, "expert", up_pairs),
            lax.ppermute(downward, "expert", down_pairs),
        )

    def across(value, pairs):
        def shifted(part, by):
            moves = [
                (s * experts + a, (s + by) % sections * experts + b)
                for s in range(sections)
                for a, b in pairs
            ]
            return lax.ppermute(part, ("section", "expert"), moves)

        if sections == 2:
            return shifted(value, 1)
        parts = [shifted(value[:, :width], 1), shifted(value[:, width:], -1)]
        return jnp.concatenate(parts, axis=1)

    message, rest = call(
        functools.partial(pack_kernel, experts),
        "pack",
        [((tokens, 3 * width + lanes), BF16), ((tokens, 3 * width), BF16)],
        front_rows[0],
        front_routes[0].T,
        front_weights[0].T,
        rear_rows[0],
        rear_routes[0].T,
        rear_weights[0].T,
        rear_cotangent[0],
        norm_gain,
        limit=PACK_LIMIT,
    )
    def after(value, *first):
        return lax.optimization_barrier((value, *first))[0]

    weights = [gate_weight[0, 0], up_weight[0, 0], down_weight[0, 0]]
    held = call(
        hold_kernel,
        "hold",
        [(weight.shape, weight.dtype) for weight in weights],
        *[after(weight, message) for weight in weights],
        limit=HOLD_LIMIT,
        scratch=[pltpu.SemaphoreType.DMA((len(weights),))],
        anywhere=range(len(weights)),
    )
    moved = [lax.ppermute(after(weight, message), "expert", twin_pairs) for weight in weights]
    held = [*held, *moved]

    def expert_of(*parts):
        rows = sum(part.shape[0] for part in parts)
        return call(
            functools.partial(expert_kernel, experts),
            "expert",
            [((rows, 2 * width), F32)],
            *parts,
            *held,
            norm_gain,
            flops=2 * 2 * rows * 8 * weights[0].size,
        )[0]

    below, above = both(message, message)
    here = [(i, i) for i in range(experts)]
    rest = across(after(rest, *held[: len(weights)]), here)
    results = []
    for step in range(1, reach):
        below = after(below, *(results[-1:] or held[: len(weights)]))
        above = after(above, below)
        mine = (below, above)
        if step == reach - 2:
            mine = (after(below, rest), above)
        if step == reach - 1:
            mine = (after(below, home), above)
        if step < reach - 1:
            below, above = both(below, above)
        else:
            below, above = both(below[:half], above[half:])
        results.append(expert_of(*mine, *([message] if step == 1 else [])))
        if step == 1:
            home = across(results[0][2 * tokens :].astype(BF16), here)
    from_below = from_above = None
    for step in range(reach - 1, 0, -1):
        to_above = results[step - 1][tokens : 2 * tokens]
        to_below = results[step - 1][:tokens]
        if step < reach - 1:
            to_above = to_above + from_below.astype(F32)
        to_above = to_above.astype(BF16)
        if step == reach - 2:
            to_above = after(to_above, far)
        if step < reach - 1:
            from_above = after(from_above, to_above)
            to_below = to_below + from_above.astype(F32)
        to_below = to_below.astype(BF16)
        if step == reach - 1:
            far = expert_of(after(below, to_above, to_below), above).astype(BF16)
        if step == reach - 2:
            far = across(after(far, to_below), ring_pairs(experts, reach))
        if step > 1:
            from_below, from_above = both(to_above, to_below)
    from_below, from_above = across(to_above, up_pairs), across(to_below, down_pairs)
    front, rear = call(
        finish_kernel, "finish", [((tokens, width), BF16)] * 2, rest, home, far, from_below, from_above
    )
    return (front[None], rear[None])


def solution(mesh):
    rows = P("section", "expert", None)
    weights = P("section", "expert", None, None)
    placed = (rows,) * 7 + (P("section", None),) + (weights,) * 3
    return jax.shard_map(
        shards, mesh=mesh, in_specs=placed, out_specs=(rows, rows), check_vma=False
    )
```

```python
import functools

import jax
import jax.numpy as jnp
from jax import lax
from jax.experimental import pallas as pl
from jax.experimental.pallas import tpu as pltpu
from jax.sharding import PartitionSpec as P

epsilon = 1e-06
F32 = jnp.float32
BF16 = jnp.bfloat16
VMEM_LIMIT = 16 * 1024 * 1024
PACK_LIMIT = 60 * 1024 * 1024
HOLD_LIMIT = 50 * 1024 * 1024


def call(kernel, name, shapes, *operands, scalars=0, flops=0, limit=VMEM_LIMIT, scratch=(), anywhere=()):
    vmem = pl.BlockSpec(memory_space=pltpu.VMEM)
    smem = pl.BlockSpec(memory_space=pltpu.SMEM)
    places = [smem] * scalars + [vmem] * (len(operands) - scalars)
    for at in anywhere:
        places[at] = pl.BlockSpec(memory_space=pltpu.HBM)
    shapes = [jax.ShapeDtypeStruct(shape, dtype) for shape, dtype in shapes]
    moved = sum(value.size * value.dtype.itemsize for value in [*operands, *shapes])
    return pl.pallas_call(
        kernel,
        out_shape=shapes,
        in_specs=places,
        out_specs=[vmem] * len(shapes),
        scratch_shapes=scratch,
        compiler_params=pltpu.CompilerParams(vmem_limit_bytes=limit),
        cost_estimate=pl.CostEstimate(flops=flops, bytes_accessed=moved, transcendentals=0),
        name=name,
    )(*operands)


def ring_of(experts):
    chips = experts // 2
    return list(range(0, chips, 2)) + list(range(1, chips, 2))[::-1]


def ring_pairs(experts, by):
    ring = ring_of(experts)
    chips = len(ring)
    return [
        (2 * ring[i] + c, 2 * ring[(i + by) % chips] + c) for i in range(chips) for c in range(2)
    ]


def table_lanes(experts):
    return -(-4 * experts // 128) * 128


def pack_kernel(experts, fr, frt, fw, rr, rrt, rw, ct, gain, msg):
    tokens, width = fr.shape
    lanes = table_lanes(experts)
    for j, rows in ((0, fr), (1, rr)):
        wide = rows[...].astype(F32)
        inverse = lax.rsqrt(jnp.mean(wide * wide, axis=-1, keepdims=True) + epsilon)
        msg[:, j * width : (j + 1) * width] = (wide * inverse * gain[...]).astype(BF16)
    msg[:, 2 * width : 3 * width] = ct[...]
    row = lax.broadcasted_iota(jnp.int32, (lanes, tokens), 0)
    table = jnp.zeros((lanes, tokens), F32)
    for group, (routes, weights) in enumerate(((frt, fw), (frt, fw), (rrt, rw), (rrt, rw))):
        for k in range(routes.shape[0]):
            hit = row == routes[k : k + 1, :] + group * experts
            weight = weights[k : k + 1, :]
            high = weight.astype(BF16).astype(F32)
            table = table + jnp.where(hit, high if group % 2 == 0 else weight - high, 0.0)
    msg[:, 3 * width :] = table.T.astype(BF16)


def sigmoid(v):
    return 1.0 / (1.0 + jnp.exp(-v))


def hold_kernel(*refs):
    *refs, sems = refs
    count = len(refs) // 2
    copies = [
        pltpu.make_async_copy(refs[i], refs[count + i], sems.at[i]) for i in range(count)
    ]
    for copy in copies:
        copy.start()
    for copy in copies:
        copy.wait()


def expert_kernel(experts, *refs):
    *parts, gate, up, down, gate_twin, up_twin, down_twin, gain, out = refs
    width = gate.shape[0]
    rows = jnp.concatenate([part[:, : 3 * width] for part in parts], axis=0)
    table = jnp.concatenate([part[:, 3 * width :] for part in parts], axis=0).astype(F32)
    lane = lax.broadcasted_iota(jnp.int32, table.shape, 1)
    count = rows.shape[0]
    across = (((1,), (1,)), ((), ()))

    def mixing(expert, group):
        hit = (lane == expert + group * experts) | (lane == expert + (group + 1) * experts)
        return jnp.sum(jnp.where(hit, table, 0.0), axis=-1, keepdims=True)

    def dot(a, b):
        return jnp.dot(a, b, preferred_element_type=F32)

    def dot_t(a, b):
        return lax.dot_general(a, b, across, preferred_element_type=F32)

    both_rows = jnp.concatenate([rows[:, :width], rows[:, width : 2 * width]], axis=0)
    cotangent = rows[:, 2 * width :]
    me = lax.axis_index("expert")
    front = rear = 0.0
    for expert, gate, up, down in (
        (me, gate, up, down),
        (me ^ 1, gate_twin, up_twin, down_twin),
    ):
        gate_value = dot(both_rows, gate[...])
        up_value = dot(both_rows, up[...])
        g = sigmoid(gate_value)
        silu = gate_value * g
        hidden = (silu[:count] * up_value[:count]).astype(BF16)
        front = front + dot(hidden, down[...]) * mixing(expert, 0)
        gate_value, up_value, g, silu = (v[count:] for v in (gate_value, up_value, g, silu))
        hidden_grad = dot_t(cotangent, down[...]) * mixing(expert, 2)
        gate_grad = (hidden_grad * up_value * g * (1.0 + gate_value * (1.0 - g))).astype(BF16)
        up_grad = (hidden_grad * silu).astype(BF16)
        rear = rear + dot_t(gate_grad, gate[...]) + dot_t(up_grad, up[...])
    out[:, :width] = front
    out[:, width:] = rear * gain[...]


def finish_kernel(home, far, below, above, front, rear):
    width = front.shape[1]
    own, rows, own_grad, rear_rows, cotangent = (
        home[:, j * width : (j + 1) * width].astype(F32) for j in range(5)
    )
    total = far[...].astype(F32) + below[...].astype(F32) + above[...].astype(F32)
    front[...] = (rows + (own + total[:, :width])).astype(BF16)
    inverse = lax.rsqrt(jnp.mean(rear_rows * rear_rows, axis=-1, keepdims=True) + epsilon)
    grad = own_grad + total[:, width:]
    along = jnp.mean(rear_rows * grad, axis=-1, keepdims=True)
    cubed = inverse * inverse * inverse
    rear[...] = (cotangent + inverse * grad - rear_rows * cubed * along).astype(BF16)


def shards(
    front_rows,
    front_routes,
    front_weights,
    rear_rows,
    rear_routes,
    rear_weights,
    rear_cotangent,
    norm_gain,
    gate_weight,
    up_weight,
    down_weight,
):
    experts = lax.axis_size("expert")
    sections = lax.axis_size("section")
    tokens, width = front_rows.shape[1:]
    reach = experts // 4
    lanes = table_lanes(experts)
    up_pairs, down_pairs = ring_pairs(experts, 1), ring_pairs(experts, -1)
    twin_pairs = [(i, i ^ 1) for i in range(experts)]

    def both(upward, downward):
        return (
            lax.ppermute(upward, "expert", up_pairs),
            lax.ppermute(downward, "expert", down_pairs),
        )

    def across(value, pairs, ahead):
        def shifted(part, by):
            moves = [
                (s * experts + a, (s + by) % sections * experts + b)
                for s in range(sections)
                for a, b in pairs
            ]
            return lax.ppermute(part, ("section", "expert"), moves)

        if sections == 2:
            return shifted(value, 1)
        parts = [shifted(value[:, :ahead], 1), shifted(value[:, ahead:], -1)]
        return jnp.concatenate(parts, axis=1)

    (message,) = call(
        functools.partial(pack_kernel, experts),
        "pack",
        [((tokens, 3 * width + lanes), BF16)],
        front_rows[0],
        front_routes[0].T,
        front_weights[0].T,
        rear_rows[0],
        rear_routes[0].T,
        rear_weights[0].T,
        rear_cotangent[0],
        norm_gain,
        limit=PACK_LIMIT,
    )
    def after(value, *first):
        return lax.optimization_barrier((value, *first))[0]

    weights = [gate_weight[0, 0], up_weight[0, 0], down_weight[0, 0]]
    kept = [*weights, front_rows[0], rear_rows[0], rear_cotangent[0]]
    *held, rows, rear, cotangent = call(
        hold_kernel,
        "hold",
        [(value.shape, value.dtype) for value in kept],
        *[after(value, message) for value in kept],
        limit=HOLD_LIMIT,
        flops=20000000000,
        scratch=[pltpu.SemaphoreType.DMA((len(kept),))],
        anywhere=range(len(kept)),
    )
    moved = [lax.ppermute(after(weight, message), "expert", twin_pairs) for weight in weights]
    held = [*held, *moved]

    def expert_of(*parts):
        rows = sum(part.shape[0] for part in parts)
        return call(
            functools.partial(expert_kernel, experts),
            "expert",
            [((rows, 2 * width), F32)],
            *parts,
            *held,
            norm_gain,
            flops=2 * 2 * rows * 8 * weights[0].size,
        )[0]

    below, above = both(message, message)
    here = [(i, i) for i in range(experts)]
    results = []
    for step in range(1, reach):
        below = after(below, *(results[-1:] or held[: len(weights)]))
        above = after(above, below)
        mine = (below, above)
        if step < reach - 1:
            below, above = both(below, above)
        else:
            below = lax.ppermute(below, "expert", up_pairs)
        results.append(expert_of(*mine, *([message] if step == 1 else [])))
        if step == 1:
            home = results[0][2 * tokens :].astype(BF16)
            home = [home[:, :width], rows, home[:, width:], rear, cotangent]
            home = across(jnp.concatenate(home, axis=1), here, 2 * width)
    from_below = from_above = None
    for step in range(reach - 1, 0, -1):
        to_above = results[step - 1][tokens : 2 * tokens]
        to_below = results[step - 1][:tokens]
        if step < reach - 1:
            to_above = to_above + from_below.astype(F32)
        to_above = to_above.astype(BF16)
        if step == reach - 1:
            to_above = after(to_above, home)
        if step == reach - 2:
            to_above = after(to_above, far)
        if step < reach - 1:
            from_above = after(from_above, to_above)
            to_below = to_below + from_above.astype(F32)
        to_below = to_below.astype(BF16)
        if step == reach - 1:
            far = expert_of(after(below, to_above, to_below)).astype(BF16)
        if step == reach - 2:
            far = across(after(far, to_below), ring_pairs(experts, reach), width)
        if step > 1:
            from_below, from_above = both(to_above, to_below)
    from_below, from_above = across(to_above, up_pairs, width), across(to_below, down_pairs, width)
    front, rear = call(
        finish_kernel, "finish", [((tokens, width), BF16)] * 2, home, far, from_below, from_above
    )
    return (front[None], rear[None])


def solution(mesh):
    rows = P("section", "expert", None)
    weights = P("section", "expert", None, None)
    placed = (rows,) * 7 + (P("section", None),) + (weights,) * 3
    return jax.shard_map(
        shards, mesh=mesh, in_specs=placed, out_specs=(rows, rows), check_vma=False
    )
```

```python
import functools

import jax
import jax.numpy as jnp
from jax import lax
from jax.experimental import pallas as pl
from jax.experimental.pallas import tpu as pltpu
from jax.sharding import PartitionSpec as P

epsilon = 1e-06
F32 = jnp.float32
BF16 = jnp.bfloat16
VMEM_LIMIT = 16 * 1024 * 1024
PACK_LIMIT = 60 * 1024 * 1024
HOLD_LIMIT = 47 * 1024 * 1024


def call(kernel, name, shapes, *operands, scalars=0, flops=0, limit=VMEM_LIMIT, scratch=(), anywhere=()):
    vmem = pl.BlockSpec(memory_space=pltpu.VMEM)
    smem = pl.BlockSpec(memory_space=pltpu.SMEM)
    places = [smem] * scalars + [vmem] * (len(operands) - scalars)
    for at in anywhere:
        places[at] = pl.BlockSpec(memory_space=pltpu.HBM)
    shapes = [jax.ShapeDtypeStruct(shape, dtype) for shape, dtype in shapes]
    moved = sum(value.size * value.dtype.itemsize for value in [*operands, *shapes])
    return pl.pallas_call(
        kernel,
        out_shape=shapes,
        in_specs=places,
        out_specs=[vmem] * len(shapes),
        scratch_shapes=scratch,
        compiler_params=pltpu.CompilerParams(vmem_limit_bytes=limit),
        cost_estimate=pl.CostEstimate(flops=flops, bytes_accessed=moved, transcendentals=0),
        name=name,
    )(*operands)


def ring_of(experts):
    chips = experts // 2
    return list(range(0, chips, 2)) + list(range(1, chips, 2))[::-1]


def ring_pairs(experts, by):
    ring = ring_of(experts)
    chips = len(ring)
    return [
        (2 * ring[i] + c, 2 * ring[(i + by) % chips] + c) for i in range(chips) for c in range(2)
    ]


def table_lanes(experts):
    return -(-4 * experts // 128) * 128


def pack_kernel(experts, fr, frt, fw, rr, rrt, rw, ct, gain, msg):
    tokens, width = fr.shape
    lanes = table_lanes(experts)
    for j, rows in ((0, fr), (1, rr)):
        wide = rows[...].astype(F32)
        inverse = lax.rsqrt(jnp.mean(wide * wide, axis=-1, keepdims=True) + epsilon)
        msg[:, j * width : (j + 1) * width] = (wide * inverse * gain[...]).astype(BF16)
    msg[:, 2 * width : 3 * width] = ct[...]
    row = lax.broadcasted_iota(jnp.int32, (lanes, tokens), 0)
    table = jnp.zeros((lanes, tokens), F32)
    for group, (routes, weights) in enumerate(((frt, fw), (frt, fw), (rrt, rw), (rrt, rw))):
        for k in range(routes.shape[0]):
            hit = row == routes[k : k + 1, :] + group * experts
            weight = weights[k : k + 1, :]
            high = weight.astype(BF16).astype(F32)
            table = table + jnp.where(hit, high if group % 2 == 0 else weight - high, 0.0)
    msg[:, 3 * width :] = table.T.astype(BF16)


def sigmoid(v):
    return 1.0 / (1.0 + jnp.exp(-v))


def hold_kernel(count, *refs):
    *refs, sems = refs
    copies = [
        pltpu.make_async_copy(refs[i], refs[count + i], sems.at[i]) for i in range(count)
    ]
    for copy in copies:
        copy.start()
    for i, copy in enumerate(copies):
        copy.wait()
        if 2 * count + i < len(refs):
            refs[2 * count + i][...] = refs[count + i][...].T


def first_kernel(experts, *refs):
    *refs, gain, out, gate_twin_t, up_twin_t, down_twin_t = refs
    turned = (gate_twin_t, up_twin_t, down_twin_t)
    for source, target in zip(refs[-3:], turned):
        target[...] = source[...].T
    expert_kernel(experts, *refs, *turned, gain, out)


def expert_kernel(experts, *refs):
    *parts, gate, up, down, gate_t, up_t, down_t = refs[:-8]
    gate_twin, up_twin, down_twin, gate_twin_t, up_twin_t, down_twin_t, gain, out = refs[-8:]
    width = gate.shape[0]
    rows = jnp.concatenate([part[:, : 3 * width] for part in parts], axis=0)
    table = jnp.concatenate([part[:, 3 * width :] for part in parts], axis=0).astype(F32)
    lane = lax.broadcasted_iota(jnp.int32, table.shape, 1)
    count = rows.shape[0]

    def mixing(expert, group):
        hit = (lane == expert + group * experts) | (lane == expert + (group + 1) * experts)
        return jnp.sum(jnp.where(hit, table, 0.0), axis=-1, keepdims=True)

    def dot(a, b):
        return jnp.dot(a, b, preferred_element_type=F32)

    both_rows = jnp.concatenate([rows[:, :width], rows[:, width : 2 * width]], axis=0)
    cotangent = rows[:, 2 * width :]
    me = lax.axis_index("expert")
    front = rear = 0.0
    for expert, gate, up, down, turned in (
        (me, gate, up, down, (gate_t, up_t, down_t)),
        (me ^ 1, gate_twin, up_twin, down_twin, (gate_twin_t, up_twin_t, down_twin_t)),
    ):
        gate_value = dot(both_rows, gate[...])
        up_value = dot(both_rows, up[...])
        g = sigmoid(gate_value)
        silu = gate_value * g
        hidden = (silu[:count] * up_value[:count]).astype(BF16)
        front = front + dot(hidden, down[...]) * mixing(expert, 0)
        gate_value, up_value, g, silu = (v[count:] for v in (gate_value, up_value, g, silu))
        hidden_grad = dot(cotangent, turned[2][...]) * mixing(expert, 2)
        gate_grad = (hidden_grad * up_value * g * (1.0 + gate_value * (1.0 - g))).astype(BF16)
        up_grad = (hidden_grad * silu).astype(BF16)
        rear = rear + dot(gate_grad, turned[0][...]) + dot(up_grad, turned[1][...])
    out[:, :width] = front
    out[:, width:] = rear * gain[...]


def finish_kernel(home, far, below, above, front, rear):
    width = front.shape[1]
    own, rows, own_grad, rear_rows, cotangent = (
        home[:, j * width : (j + 1) * width].astype(F32) for j in range(5)
    )
    total = far[...].astype(F32) + below[...].astype(F32) + above[...].astype(F32)
    front[...] = (rows + (own + total[:, :width])).astype(BF16)
    inverse = lax.rsqrt(jnp.mean(rear_rows * rear_rows, axis=-1, keepdims=True) + epsilon)
    grad = own_grad + total[:, width:]
    along = jnp.mean(rear_rows * grad, axis=-1, keepdims=True)
    cubed = inverse * inverse * inverse
    rear[...] = (cotangent + inverse * grad - rear_rows * cubed * along).astype(BF16)


def shards(
    front_rows,
    front_routes,
    front_weights,
    rear_rows,
    rear_routes,
    rear_weights,
    rear_cotangent,
    norm_gain,
    gate_weight,
    up_weight,
    down_weight,
):
    experts = lax.axis_size("expert")
    sections = lax.axis_size("section")
    tokens, width = front_rows.shape[1:]
    reach = experts // 4
    lanes = table_lanes(experts)
    up_pairs, down_pairs = ring_pairs(experts, 1), ring_pairs(experts, -1)
    twin_pairs = [(i, i ^ 1) for i in range(experts)]

    def both(upward, downward):
        return (
            lax.ppermute(upward, "expert", up_pairs),
            lax.ppermute(downward, "expert", down_pairs),
        )

    def across(value, pairs, ahead):
        def shifted(part, by):
            moves = [
                (s * experts + a, (s + by) % sections * experts + b)
                for s in range(sections)
                for a, b in pairs
            ]
            return lax.ppermute(part, ("section", "expert"), moves)

        if sections == 2:
            return shifted(value, 1)
        parts = [shifted(value[:, :ahead], 1), shifted(value[:, ahead:], -1)]
        return jnp.concatenate(parts, axis=1)

    (message,) = call(
        functools.partial(pack_kernel, experts),
        "pack",
        [((tokens, 3 * width + lanes), BF16)],
        front_rows[0],
        front_routes[0].T,
        front_weights[0].T,
        rear_rows[0],
        rear_routes[0].T,
        rear_weights[0].T,
        rear_cotangent[0],
        norm_gain,
        limit=PACK_LIMIT,
    )
    def after(value, *first):
        return lax.optimization_barrier((value, *first))[0]

    weights = [gate_weight[0, 0], up_weight[0, 0], down_weight[0, 0]]
    kept = [*weights, front_rows[0], rear_rows[0], rear_cotangent[0]]
    held = call(
        functools.partial(hold_kernel, len(kept)),
        "hold",
        [(value.shape, value.dtype) for value in kept]
        + [(weight.shape[::-1], weight.dtype) for weight in weights],
        *[after(value, message) for value in kept],
        limit=HOLD_LIMIT,
        flops=20000000000,
        scratch=[pltpu.SemaphoreType.DMA((len(kept),))],
        anywhere=range(len(kept)),
    )
    rows, rear, cotangent = held[3:6]
    held = [*held[:3], *held[6:]]
    moved = [lax.ppermute(after(weight, message), "expert", twin_pairs) for weight in weights]
    held = [*held, *moved]

    def expert_of(*parts):
        rows = sum(part.shape[0] for part in parts)
        first = len(held) < 4 * len(weights)
        kernel = first_kernel if first else expert_kernel
        turned = [(weight.shape[::-1], weight.dtype) for weight in weights]
        result, *new = call(
            functools.partial(kernel, experts),
            "expert",
            [((rows, 2 * width), F32)] + (turned if first else []),
            *parts,
            *held,
            norm_gain,
            flops=2 * 2 * rows * 8 * weights[0].size,
        )
        held.extend(new)
        return result

    below, above = both(message, message)
    here = [(i, i) for i in range(experts)]
    results = []
    for step in range(1, reach):
        below = after(below, *(results[-1:] or held[: 2 * len(weights)]))
        above = after(above, below)
        mine = (below, above)
        if step < reach - 1:
            below, above = both(below, above)
        else:
            below = lax.ppermute(below, "expert", up_pairs)
        results.append(expert_of(*mine, *([message] if step == 1 else [])))
        if step == 1:
            home = results[0][2 * tokens :].astype(BF16)
            home = [home[:, :width], rows, home[:, width:], rear, cotangent]
            home = across(jnp.concatenate(home, axis=1), here, 2 * width)
    from_below = from_above = None
    for step in range(reach - 1, 0, -1):
        to_above = results[step - 1][tokens : 2 * tokens]
        to_below = results[step - 1][:tokens]
        if step < reach - 1:
            to_above = to_above + from_below.astype(F32)
        to_above = to_above.astype(BF16)
        if step == reach - 1:
            to_above = after(to_above, home)
        if step == reach - 2:
            to_above = after(to_above, far)
        if step < reach - 1:
            from_above = after(from_above, to_above)
            to_below = to_below + from_above.astype(F32)
        to_below = to_below.astype(BF16)
        if step == reach - 1:
            far = expert_of(after(below, to_above, to_below)).astype(BF16)
        if step == reach - 2:
            far = across(after(far, to_below), ring_pairs(experts, reach), width)
        if step > 1:
            from_below, from_above = both(to_above, to_below)
    from_below, from_above = across(to_above, up_pairs, width), across(to_below, down_pairs, width)
    front, rear = call(
        finish_kernel, "finish", [((tokens, width), BF16)] * 2, home, far, from_below, from_above
    )
    return (front[None], rear[None])


def solution(mesh):
    rows = P("section", "expert", None)
    weights = P("section", "expert", None, None)
    placed = (rows,) * 7 + (P("section", None),) + (weights,) * 3
    return jax.shard_map(
        shards, mesh=mesh, in_specs=placed, out_specs=(rows, rows), check_vma=False
    )
```

```python
import functools

import jax
import jax.numpy as jnp
from jax import lax
from jax.experimental import pallas as pl
from jax.experimental.pallas import tpu as pltpu
from jax.sharding import PartitionSpec as P

epsilon = 1e-06
F32 = jnp.float32
BF16 = jnp.bfloat16
VMEM_LIMIT = 16 * 1024 * 1024
PACK_LIMIT = 60 * 1024 * 1024
HOLD_LIMIT = 47 * 1024 * 1024


def call(kernel, name, shapes, *operands, scalars=0, flops=0, limit=VMEM_LIMIT, scratch=(), anywhere=()):
    vmem = pl.BlockSpec(memory_space=pltpu.VMEM)
    smem = pl.BlockSpec(memory_space=pltpu.SMEM)
    places = [smem] * scalars + [vmem] * (len(operands) - scalars)
    for at in anywhere:
        places[at] = pl.BlockSpec(memory_space=pltpu.HBM)
    shapes = [jax.ShapeDtypeStruct(shape, dtype) for shape, dtype in shapes]
    moved = sum(value.size * value.dtype.itemsize for value in [*operands, *shapes])
    return pl.pallas_call(
        kernel,
        out_shape=shapes,
        in_specs=places,
        out_specs=[vmem] * len(shapes),
        scratch_shapes=scratch,
        compiler_params=pltpu.CompilerParams(vmem_limit_bytes=limit),
        cost_estimate=pl.CostEstimate(flops=flops, bytes_accessed=moved, transcendentals=0),
        name=name,
    )(*operands)


def ring_of(experts):
    chips = experts // 2
    return list(range(0, chips, 2)) + list(range(1, chips, 2))[::-1]


def ring_pairs(experts, by):
    ring = ring_of(experts)
    chips = len(ring)
    return [
        (2 * ring[i] + c, 2 * ring[(i + by) % chips] + c) for i in range(chips) for c in range(2)
    ]


def table_lanes(experts):
    return -(-4 * experts // 128) * 128


def pack_kernel(experts, fr, frt, fw, rr, rrt, rw, ct, gain, msg):
    tokens, width = fr.shape
    lanes = table_lanes(experts)
    for j, rows in ((0, fr), (1, rr)):
        wide = rows[...].astype(F32)
        inverse = lax.rsqrt(jnp.mean(wide * wide, axis=-1, keepdims=True) + epsilon)
        msg[:, j * width : (j + 1) * width] = (wide * inverse * gain[...]).astype(BF16)
    msg[:, 2 * width : 3 * width] = ct[...]
    expert = lax.broadcasted_iota(jnp.int32, (experts, tokens), 0)
    table = []
    for routes, weights in ((frt, fw), (rrt, rw)):
        mixing = jnp.zeros((experts, tokens), F32)
        for k in range(routes.shape[0]):
            mixing += jnp.where(expert == routes[k : k + 1, :], weights[k : k + 1, :], 0.0)
        high = mixing.astype(BF16).astype(F32)
        table += [high, mixing - high]
    table.append(jnp.zeros((lanes - 4 * experts, tokens), F32))
    table = jnp.concatenate(table[: 4 if lanes == 4 * experts else 5], axis=0)
    msg[:, 3 * width :] = table.T.astype(BF16)


def sigmoid(v):
    return 1.0 / (1.0 + jnp.exp(-v))


def hold_kernel(count, *refs):
    *refs, sems = refs
    copies = [
        pltpu.make_async_copy(refs[i], refs[count + i], sems.at[i]) for i in range(count)
    ]
    for copy in copies:
        copy.start()
    for i, copy in enumerate(copies):
        copy.wait()
        if 2 * count + i < len(refs):
            refs[2 * count + i][...] = refs[count + i][...].T


def first_kernel(experts, *refs):
    *refs, gain, out, gate_twin_t, up_twin_t, down_twin_t = refs
    turned = (gate_twin_t, up_twin_t, down_twin_t)
    for source, target in zip(refs[-3:], turned):
        target[...] = source[...].T
    expert_kernel(experts, *refs, *turned, gain, out)


def expert_kernel(experts, *refs):
    *parts, gate, up, down, gate_t, up_t, down_t = refs[:-8]
    gate_twin, up_twin, down_twin, gate_twin_t, up_twin_t, down_twin_t, gain, out = refs[-8:]
    width = gate.shape[0]
    rows = jnp.concatenate([part[:, : 3 * width] for part in parts], axis=0)
    table = jnp.concatenate([part[:, 3 * width :] for part in parts], axis=0).astype(F32)
    lane = lax.broadcasted_iota(jnp.int32, table.shape, 1)
    count = rows.shape[0]

    def mixing(expert, group):
        hit = (lane == expert + group * experts) | (lane == expert + (group + 1) * experts)
        return jnp.sum(jnp.where(hit, table, 0.0), axis=-1, keepdims=True)

    def dot(a, b):
        return jnp.dot(a, b, preferred_element_type=F32)

    both_rows = jnp.concatenate([rows[:, :width], rows[:, width : 2 * width]], axis=0)
    cotangent = rows[:, 2 * width :]
    me = lax.axis_index("expert")
    front = rear = 0.0
    for expert, gate, up, down, turned in (
        (me, gate, up, down, (gate_t, up_t, down_t)),
        (me ^ 1, gate_twin, up_twin, down_twin, (gate_twin_t, up_twin_t, down_twin_t)),
    ):
        gate_value = dot(both_rows, gate[...])
        up_value = dot(both_rows, up[...])
        g = sigmoid(gate_value)
        silu = gate_value * g
        hidden = (silu[:count] * up_value[:count]).astype(BF16)
        front = front + dot(hidden, down[...]) * mixing(expert, 0)
        gate_value, up_value, g, silu = (v[count:] for v in (gate_value, up_value, g, silu))
        hidden_grad = dot(cotangent, turned[2][...]) * mixing(expert, 2)
        gate_grad = (hidden_grad * up_value * g * (1.0 + gate_value * (1.0 - g))).astype(BF16)
        up_grad = (hidden_grad * silu).astype(BF16)
        rear = rear + dot(gate_grad, turned[0][...]) + dot(up_grad, turned[1][...])
    out[:, :width] = front.astype(out.dtype)
    out[:, width:] = (rear * gain[...]).astype(out.dtype)


def finish_kernel(home, far, below, above, front, rear):
    width = front.shape[1]
    own, rows, own_grad, rear_rows, cotangent = (
        home[:, j * width : (j + 1) * width].astype(F32) for j in range(5)
    )
    total = far[...].astype(F32) + below[...].astype(F32) + above[...].astype(F32)
    front[...] = (rows + (own + total[:, :width])).astype(BF16)
    inverse = lax.rsqrt(jnp.mean(rear_rows * rear_rows, axis=-1, keepdims=True) + epsilon)
    grad = own_grad + total[:, width:]
    along = jnp.mean(rear_rows * grad, axis=-1, keepdims=True)
    cubed = inverse * inverse * inverse
    rear[...] = (cotangent + inverse * grad - rear_rows * cubed * along).astype(BF16)


def shards(
    front_rows,
    front_routes,
    front_weights,
    rear_rows,
    rear_routes,
    rear_weights,
    rear_cotangent,
    norm_gain,
    gate_weight,
    up_weight,
    down_weight,
):
    experts = lax.axis_size("expert")
    sections = lax.axis_size("section")
    tokens, width = front_rows.shape[1:]
    reach = experts // 4
    lanes = table_lanes(experts)
    up_pairs, down_pairs = ring_pairs(experts, 1), ring_pairs(experts, -1)
    twin_pairs = [(i, i ^ 1) for i in range(experts)]

    def both(upward, downward):
        return (
            lax.ppermute(upward, "expert", up_pairs),
            lax.ppermute(downward, "expert", down_pairs),
        )

    def across(value, pairs, ahead):
        def shifted(part, by):
            moves = [
                (s * experts + a, (s + by) % sections * experts + b)
                for s in range(sections)
                for a, b in pairs
            ]
            return lax.ppermute(part, ("section", "expert"), moves)

        if sections == 2:
            return shifted(value, 1)
        parts = [shifted(value[:, :ahead], 1), shifted(value[:, ahead:], -1)]
        return jnp.concatenate(parts, axis=1)

    (message,) = call(
        functools.partial(pack_kernel, experts),
        "pack",
        [((tokens, 3 * width + lanes), BF16)],
        front_rows[0],
        front_routes[0].T,
        front_weights[0].T,
        rear_rows[0],
        rear_routes[0].T,
        rear_weights[0].T,
        rear_cotangent[0],
        norm_gain,
        limit=PACK_LIMIT,
    )
    def after(value, *first):
        return lax.optimization_barrier((value, *first))[0]

    weights = [gate_weight[0, 0], up_weight[0, 0], down_weight[0, 0]]
    kept = [*weights, front_rows[0], rear_rows[0], rear_cotangent[0]]
    held = call(
        functools.partial(hold_kernel, len(kept)),
        "hold",
        [(value.shape, value.dtype) for value in kept]
        + [(weight.shape[::-1], weight.dtype) for weight in weights],
        *[after(value, message) for value in kept],
        limit=HOLD_LIMIT,
        flops=20000000000,
        scratch=[pltpu.SemaphoreType.DMA((len(kept),))],
        anywhere=range(len(kept)),
    )
    rows, rear, cotangent = held[3:6]
    held = [*held[:3], *held[6:]]
    moved = [lax.ppermute(after(weight, message), "expert", twin_pairs) for weight in weights]
    held = [*held, *moved]

    def expert_of(*parts, dtype=F32):
        rows = sum(part.shape[0] for part in parts)
        first = len(held) < 4 * len(weights)
        kernel = first_kernel if first else expert_kernel
        turned = [(weight.shape[::-1], weight.dtype) for weight in weights]
        result, *new = call(
            functools.partial(kernel, experts),
            "expert",
            [((rows, 2 * width), dtype)] + (turned if first else []),
            *parts,
            *held,
            norm_gain,
            flops=2 * 2 * rows * 8 * weights[0].size,
        )
        held.extend(new)
        return result

    below, above = both(message, message)
    here = [(i, i) for i in range(experts)]
    results = []
    for step in range(1, reach):
        below = after(below, *(results[-1:] or held[: 2 * len(weights)]))
        above = after(above, below)
        mine = (below, above)
        if step < reach - 1:
            below, above = both(below, above)
        else:
            below = lax.ppermute(below, "expert", up_pairs)
        results.append(expert_of(*mine, *([message] if step == 1 else [])))
        if step == 1:
            home = results[0][2 * tokens :].astype(BF16)
            home = [home[:, :width], rows, home[:, width:], rear, cotangent]
            home = across(jnp.concatenate(home, axis=1), here, 2 * width)
    from_below = from_above = None
    for step in range(reach - 1, 0, -1):
        to_above = results[step - 1][tokens : 2 * tokens]
        to_below = results[step - 1][:tokens]
        if step < reach - 1:
            to_above = to_above + from_below.astype(F32)
        to_above = to_above.astype(BF16)
        if step == reach - 1:
            to_above = after(to_above, home)
        if step == reach - 2:
            to_above = after(to_above, far)
        if step < reach - 1:
            from_above = after(from_above, to_above)
            to_below = to_below + from_above.astype(F32)
        to_below = to_below.astype(BF16)
        if step == reach - 1:
            far = expert_of(after(below, to_above, to_below), dtype=BF16)
        if step == reach - 2:
            far = across(after(far, to_below), ring_pairs(experts, reach), width)
        if step > 1:
            from_below, from_above = both(to_above, to_below)
    from_below, from_above = across(to_above, up_pairs, width), across(to_below, down_pairs, width)
    front, rear = call(
        finish_kernel, "finish", [((tokens, width), BF16)] * 2, home, far, from_below, from_above
    )
    return (front[None], rear[None])


def solution(mesh):
    rows = P("section", "expert", None)
    weights = P("section", "expert", None, None)
    placed = (rows,) * 7 + (P("section", None),) + (weights,) * 3
    return jax.shard_map(
        shards, mesh=mesh, in_specs=placed, out_specs=(rows, rows), check_vma=False
    )
```

```python
import functools

import jax
import jax.numpy as jnp
from jax import lax
from jax.experimental import pallas as pl
from jax.experimental.pallas import tpu as pltpu
from jax.sharding import PartitionSpec as P

epsilon = 1e-06
F32 = jnp.float32
BF16 = jnp.bfloat16
VMEM_LIMIT = 16 * 1024 * 1024
PACK_LIMIT = 60 * 1024 * 1024
HOLD_LIMIT = 47 * 1024 * 1024


def call(kernel, name, shapes, *operands, scalars=0, flops=0, limit=VMEM_LIMIT, scratch=(), anywhere=()):
    vmem = pl.BlockSpec(memory_space=pltpu.VMEM)
    smem = pl.BlockSpec(memory_space=pltpu.SMEM)
    places = [smem] * scalars + [vmem] * (len(operands) - scalars)
    for at in anywhere:
        places[at] = pl.BlockSpec(memory_space=pltpu.HBM)
    shapes = [jax.ShapeDtypeStruct(shape, dtype) for shape, dtype in shapes]
    moved = sum(value.size * value.dtype.itemsize for value in [*operands, *shapes])
    return pl.pallas_call(
        kernel,
        out_shape=shapes,
        in_specs=places,
        out_specs=[vmem] * len(shapes),
        scratch_shapes=scratch,
        compiler_params=pltpu.CompilerParams(vmem_limit_bytes=limit),
        cost_estimate=pl.CostEstimate(flops=flops, bytes_accessed=moved, transcendentals=0),
        name=name,
    )(*operands)


def ring_of(experts):
    chips = experts // 2
    return list(range(0, chips, 2)) + list(range(1, chips, 2))[::-1]


def ring_pairs(experts, by):
    ring = ring_of(experts)
    chips = len(ring)
    return [
        (2 * ring[i] + c, 2 * ring[(i + by) % chips] + c) for i in range(chips) for c in range(2)
    ]


def table_lanes(experts):
    return -(-4 * experts // 128) * 128


def pack_kernel(experts, fr, frt, fw, rr, rrt, rw, ct, gain, msg):
    tokens, width = fr.shape
    lanes = table_lanes(experts)
    for j, rows in ((0, fr), (1, rr)):
        wide = rows[...].astype(F32)
        inverse = lax.rsqrt(jnp.mean(wide * wide, axis=-1, keepdims=True) + epsilon)
        msg[:, j * width : (j + 1) * width] = (wide * inverse * gain[...]).astype(BF16)
    msg[:, 2 * width : 3 * width] = ct[...]
    expert = lax.broadcasted_iota(jnp.int32, (experts, tokens), 0)
    table = []
    for routes, weights in ((frt, fw), (rrt, rw)):
        mixing = jnp.zeros((experts, tokens), F32)
        for k in range(routes.shape[0]):
            mixing += jnp.where(expert == routes[k : k + 1, :], weights[k : k + 1, :], 0.0)
        high = mixing.astype(BF16).astype(F32)
        table += [high, mixing - high]
    table.append(jnp.zeros((lanes - 4 * experts, tokens), F32))
    table = jnp.concatenate(table[: 4 if lanes == 4 * experts else 5], axis=0)
    msg[:, 3 * width :] = table.T.astype(BF16)


def sigmoid(v):
    return 1.0 / (1.0 + jnp.exp(-v))


def hold_kernel(count, *refs):
    *refs, sems = refs
    copies = [
        pltpu.make_async_copy(refs[i], refs[count + i], sems.at[i]) for i in range(count)
    ]
    for copy in copies:
        copy.start()
    for i, copy in enumerate(copies):
        copy.wait()
        if 2 * count + i < len(refs):
            refs[2 * count + i][...] = refs[count + i][...].T


def first_kernel(experts, *refs):
    *refs, gain, out, gate_twin_t, up_twin_t, down_twin_t = refs
    turned = (gate_twin_t, up_twin_t, down_twin_t)
    for source, target in zip(refs[-3:], turned):
        target[...] = source[...].T
    expert_kernel(experts, *refs, *turned, gain, out)


def expert_kernel(experts, *refs):
    *parts, gate, up, down, gate_t, up_t, down_t = refs[:-8]
    gate_twin, up_twin, down_twin, gate_twin_t, up_twin_t, down_twin_t, gain, out = refs[-8:]
    width = gate.shape[0]
    rows = jnp.concatenate([part[:, : 3 * width] for part in parts], axis=0)
    table = jnp.concatenate([part[:, 3 * width :] for part in parts], axis=0).astype(F32)
    lane = lax.broadcasted_iota(jnp.int32, table.shape, 1)
    count = rows.shape[0]

    def mixing(expert, group):
        hit = (lane == expert + group * experts) | (lane == expert + (group + 1) * experts)
        return jnp.sum(jnp.where(hit, table, 0.0), axis=-1, keepdims=True)

    def dot(a, b):
        return jnp.dot(a, b, preferred_element_type=F32)

    both_rows = jnp.concatenate([rows[:, :width], rows[:, width : 2 * width]], axis=0)
    cotangent = rows[:, 2 * width :]
    me = lax.axis_index("expert")
    front = rear = 0.0
    for expert, gate, up, down, turned in (
        (me, gate, up, down, (gate_t, up_t, down_t)),
        (me ^ 1, gate_twin, up_twin, down_twin, (gate_twin_t, up_twin_t, down_twin_t)),
    ):
        gate_value = dot(both_rows, gate[...])
        up_value = dot(both_rows, up[...])
        g = sigmoid(gate_value)
        silu = gate_value * g
        hidden = (silu[:count] * up_value[:count]).astype(BF16)
        front = front + dot(hidden, down[...]) * mixing(expert, 0)
        gate_value, up_value, g, silu = (v[count:] for v in (gate_value, up_value, g, silu))
        hidden_grad = dot(cotangent, turned[2][...]) * mixing(expert, 2)
        gate_grad = (hidden_grad * up_value * g * (1.0 + gate_value * (1.0 - g))).astype(BF16)
        up_grad = (hidden_grad * silu).astype(BF16)
        rear = rear + dot(gate_grad, turned[0][...]) + dot(up_grad, turned[1][...])
    out[:, :width] = front.astype(out.dtype)
    out[:, width:] = (rear * gain[...]).astype(out.dtype)


def finish_kernel(home, far, below, above, front, rear):
    width = front.shape[1]
    own, rows, own_grad, rear_rows, cotangent = (
        home[:, j * width : (j + 1) * width].astype(F32) for j in range(5)
    )
    total = far[...].astype(F32) + below[...].astype(F32) + above[...].astype(F32)
    front[...] = (rows + (own + total[:, :width])).astype(BF16)
    inverse = lax.rsqrt(jnp.mean(rear_rows * rear_rows, axis=-1, keepdims=True) + epsilon)
    grad = own_grad + total[:, width:]
    along = jnp.mean(rear_rows * grad, axis=-1, keepdims=True)
    cubed = inverse * inverse * inverse
    rear[...] = (cotangent + inverse * grad - rear_rows * cubed * along).astype(BF16)


def shards(
    front_rows,
    front_routes,
    front_weights,
    rear_rows,
    rear_routes,
    rear_weights,
    rear_cotangent,
    norm_gain,
    gate_weight,
    up_weight,
    down_weight,
):
    experts = lax.axis_size("expert")
    sections = lax.axis_size("section")
    tokens, width = front_rows.shape[1:]
    reach = experts // 4
    lanes = table_lanes(experts)
    up_pairs, down_pairs = ring_pairs(experts, 1), ring_pairs(experts, -1)
    twin_pairs = [(i, i ^ 1) for i in range(experts)]

    def both(upward, downward):
        return (
            lax.ppermute(upward, "expert", up_pairs),
            lax.ppermute(downward, "expert", down_pairs),
        )

    def across(value, pairs, ahead):
        def shifted(part, by):
            moves = [
                (s * experts + a, (s + by) % sections * experts + b)
                for s in range(sections)
                for a, b in pairs
            ]
            return lax.ppermute(part, ("section", "expert"), moves)

        if sections == 2:
            return shifted(value, 1)
        parts = [shifted(value[:, :ahead], 1), shifted(value[:, ahead:], -1)]
        return jnp.concatenate(parts, axis=1)

    (message,) = call(
        functools.partial(pack_kernel, experts),
        "pack",
        [((tokens, 3 * width + lanes), BF16)],
        front_rows[0],
        front_routes[0].T,
        front_weights[0].T,
        rear_rows[0],
        rear_routes[0].T,
        rear_weights[0].T,
        rear_cotangent[0],
        norm_gain,
        limit=PACK_LIMIT,
    )
    def after(value, *first):
        return lax.optimization_barrier((value, *first))[0]

    weights = [gate_weight[0, 0], up_weight[0, 0], down_weight[0, 0]]
    kept = [*weights, front_rows[0], rear_rows[0], rear_cotangent[0]]
    held = call(
        functools.partial(hold_kernel, len(kept)),
        "hold",
        [(value.shape, value.dtype) for value in kept]
        + [(weight.shape[::-1], weight.dtype) for weight in weights],
        *[after(value, message) for value in kept],
        limit=HOLD_LIMIT,
        flops=20000000000,
        scratch=[pltpu.SemaphoreType.DMA((len(kept),))],
        anywhere=range(len(kept)),
    )
    rows, rear, cotangent = held[3:6]
    held = [*held[:3], *held[6:]]
    moved = [lax.ppermute(after(weight, message), "expert", twin_pairs) for weight in weights]
    held = [*held, *moved]

    def expert_of(*parts, dtype=F32):
        rows = sum(part.shape[0] for part in parts)
        first = len(held) < 4 * len(weights)
        kernel = first_kernel if first else expert_kernel
        turned = [(weight.shape[::-1], weight.dtype) for weight in weights]
        result, *new = call(
            functools.partial(kernel, experts),
            "expert",
            [((rows, 2 * width), dtype)] + (turned if first else []),
            *parts,
            *held,
            norm_gain,
            flops=(1 if first else 4) * rows * 8 * weights[0].size,
        )
        held.extend(new)
        return result

    below, above = both(message, message)
    here = [(i, i) for i in range(experts)]
    results = []
    for step in range(1, reach):
        below = after(below, *(results[-1:] or held[: 2 * len(weights)]))
        above = after(above, below)
        mine = (below, above)
        if step < reach - 1:
            below, above = both(below, above)
        else:
            below = lax.ppermute(below, "expert", up_pairs)
        dtype = BF16 if step == reach - 1 else F32
        results.append(expert_of(*mine, *([message] if step == 1 else []), dtype=dtype))
        if step == 1:
            home = results[0][2 * tokens :].astype(BF16)
            home = [home[:, :width], rows, home[:, width:], rear, cotangent]
            home = across(jnp.concatenate(home, axis=1), here, 2 * width)
    from_below = from_above = None
    for step in range(reach - 1, 0, -1):
        to_above = results[step - 1][tokens : 2 * tokens]
        to_below = results[step - 1][:tokens]
        if step < reach - 1:
            to_above = to_above + from_below.astype(F32)
        to_above = to_above.astype(BF16)
        if step == reach - 1:
            to_above = after(to_above, home)
        if step == reach - 2:
            to_above = after(to_above, far)
        if step < reach - 1:
            from_above = after(from_above, to_above)
            to_below = to_below + from_above.astype(F32)
        to_below = to_below.astype(BF16)
        if step == reach - 1:
            far = expert_of(after(below, to_above, to_below), dtype=BF16)
        if step == reach - 2:
            far = across(after(far, to_below), ring_pairs(experts, reach), width)
        if step > 1:
            from_below, from_above = both(to_above, to_below)
    from_below, from_above = across(to_above, up_pairs, width), across(to_below, down_pairs, width)
    front, rear = call(
        finish_kernel, "finish", [((tokens, width), BF16)] * 2, home, far, from_below, from_above
    )
    return (front[None], rear[None])


def solution(mesh):
    rows = P("section", "expert", None)
    weights = P("section", "expert", None, None)
    placed = (rows,) * 7 + (P("section", None),) + (weights,) * 3
    return jax.shard_map(
        shards, mesh=mesh, in_specs=placed, out_specs=(rows, rows), check_vma=False
    )
```
